32 devices in a mesh: groups: 2 (over x), seg: 16 (over z, y, core).
Axes of the slice: x: 2, y: 2, z: 4, core: 2. Of those that a mesh axis runs over, the one named last changes fastest.
Arguments:
- points: bfloat16 [16, 262144], P(None, ('groups', 'seg')), parts along dimension 1, may hold values from -6 to 6
- vectors: bfloat16 [32, 262144], P(None, ('groups', 'seg')), parts along dimension 1, may hold values from -6 to 6
- lengthscale: float32 [32], P('groups'), parts along dimension 0, may hold values from 1.5 to 4
- leaf_basis: bfloat16 [512, 64, 512], P(('groups', 'seg')), parts along dimension 0, may hold values from -0.25 to 0.25
- local_transfer: bfloat16 [960, 64, 64], P(('groups', 'seg')), parts along dimension 0, may hold values from -0.625 to 0.625
- upper_transfer: bfloat16 [48, 64, 64], P('groups'), parts along dimension 0, may hold values from -0.625 to 0.625
- local_skeleton: bfloat16 [992, 16, 64], P(('groups', 'seg')), parts along dimension 0, may hold values from -6 to 6
- upper_skeleton: bfloat16 [24, 16, 64], P('groups'), parts along dimension 0, may hold values from -6 to 6
- near_offsets: int32 [512, 8], P(('groups', 'seg')), parts along dimension 0, may hold values from -8 to 8, as said below
- local_coupling: int32 [992, 4], P(('groups', 'seg')), parts along dimension 0, may hold values from -4 to 4, as said below
- upper_coupling: int32 [24, 4], P('groups'), parts along dimension 0, may hold values from -4 to 4, as said below
Outputs:
- products: float32 [32, 262144], P(None, ('groups', 'seg')), parts along dimension 1
The draws below stay inside these ranges and needn't reach their ends.
There are 2 independent parts, one for each index of `groups`. The reference program is written for one: setup_inputs(seed, part) draws one part's arguments, and reference() takes and returns one part's arrays. A program takes and returns all parts, laid end to end along the dimension named above; each array names one. Nothing has to cross between parts.
Inputs may be any that keep to these rules, and one draw needn't show every extreme that they name: `near_offsets`: each row holds 8 distinct offsets, the first of them 0. `local_coupling`: each row holds 4 distinct offsets, none of -1, 0, 1. `upper_coupling`: each row holds 4 distinct offsets, none of -1, 0, 1.
All inputs are finite; a program needn't handle non-finite values.
Results may differ from the reference program's by a relative error of at most 0.012.
Values may be sent and summed in bfloat16 or wider, within the bound.
A program may use at most 64 MiB of HBM per device.

```python
import math
import jax
import jax.numpy as jnp
from jax import lax

DIM = 16
LEAF = 512
RANK = 64
PROBES = 32
NEAR = 8
REACH = 8
CPL = 4
LEAF_DEV = 16
LEAVES = 256
NPTS = 131072
LOCAL_B = 31
LOCAL_T = 30
UPPER_B = 12
UPPER_T = 24
N_SEG = 16


def pick_offsets(key, rows, choose, span, lowest):
    number = 2 * (span - lowest + 1)
    column = jnp.arange(number, dtype=jnp.int32)
    values = jnp.where(column < number // 2, column - span, column - number // 2 + lowest)
    keys = jax.random.split(key, rows)
    orders = jax.vmap(lambda single: jax.random.permutation(single, number))(keys)[:, :choose]
    return values[orders].astype(jnp.int32)


def draw_near_offsets(key, part):
    rest = pick_offsets(jax.random.fold_in(key, 11), LEAVES, NEAR - 1, REACH, 1)
    return jnp.concatenate([jnp.zeros((LEAVES, 1), jnp.int32), rest], axis=1)


def draw_local_coupling(key, part):
    return pick_offsets(jax.random.fold_in(key, 23), N_SEG * LOCAL_B, CPL, 4, 2)


def draw_upper_coupling(key, part):
    return pick_offsets(jax.random.fold_in(key, 37), UPPER_B, CPL, 4, 2)


def block_scale(stream_key, dims, cuts, low, top_value):
    def one(axis_at, shards_of):
        draws = jax.random.uniform(jax.random.fold_in(jax.random.fold_in(stream_key, 6), axis_at), (shards_of,), jnp.float32, low / len(cuts), top_value / len(cuts))
        return jnp.repeat(jnp.exp(draws), dims[axis_at] // shards_of).reshape((-1,) + (1,) * (len(dims) - axis_at - 1))

    gain = one(*cuts[0])
    for cut in cuts[1:]:
        gain = gain * one(*cut)
    return gain


def noise(stream_key, shape, scale, bound, cuts=(), kind=jnp.bfloat16):
    values = scale * jax.random.normal(stream_key, shape, jnp.float32)
    if cuts:
        values = values * block_scale(stream_key, shape, cuts, -0.22, 0.18)
    return jnp.clip(values, -bound, bound).astype(kind)


def setup_inputs(seed: int = 0, part: int = 0) -> dict:
    streams_of = jax.random.split(jax.random.key(seed), 12)
    part_splits = jax.random.split(jax.random.fold_in(streams_of[11], part), 12)
    return {
        "points": noise(part_splits[0], (DIM, NPTS), 1.0, 6.0, ((1, 16),)),
        "vectors": noise(part_splits[1], (PROBES, NPTS), 1.0, 6.0, ((1, 16),)),
        "lengthscale": jnp.clip(jnp.exp(jax.random.uniform(part_splits[2], (DIM,), jnp.float32, math.log(1.5), math.log(4.0))), 1.5, 4.0),
        "leaf_basis": noise(part_splits[3], (LEAVES, RANK, LEAF), LEAF ** -0.5, 0.25, ((0, 16),)),
        "local_transfer": noise(part_splits[4], (N_SEG * LOCAL_T, RANK, RANK), (3 * RANK // 2) ** -0.5, 0.625, ((0, 16),)),
        "upper_transfer": noise(part_splits[5], (UPPER_T, RANK, RANK), (3 * RANK // 2) ** -0.5, 0.625),
        "local_skeleton": noise(part_splits[6], (N_SEG * LOCAL_B, DIM, RANK), 1.0, 6.0, ((0, 16),)),
        "upper_skeleton": noise(part_splits[7], (UPPER_B, DIM, RANK), 1.0, 6.0),
        "near_offsets": draw_near_offsets(jax.random.fold_in(jax.random.fold_in(streams_of[11], part), 71), part),
        "local_coupling": draw_local_coupling(jax.random.fold_in(jax.random.fold_in(streams_of[11], part), 71), part),
        "upper_coupling": draw_upper_coupling(jax.random.fold_in(jax.random.fold_in(streams_of[11], part), 71), part),
    }


def settle(values):
    return lax.optimization_barrier(values.astype(jnp.bfloat16))


def widen(values):
    return values.astype(jnp.float32)


def kernel_tiles(targets, sources, inverse_len):
    target_scaled = widen(settle(targets.astype(jnp.float32) * inverse_len[:, None]))
    source_scaled = widen(settle(sources.astype(jnp.float32) * inverse_len[:, None]))
    target_norm = jnp.sum(target_scaled * target_scaled, axis=-2)
    source_norm = jnp.sum(source_scaled * source_scaled, axis=-2)
    inner = jnp.einsum("...dm,...dk->...mk", target_scaled, source_scaled, precision=lax.Precision.HIGHEST)
    return jnp.exp(-0.5 * (target_norm[..., :, None] + source_norm[..., None, :] - 2.0 * inner))


def level_rows(array, per_device, first_row, number):
    shaped = array.reshape((N_SEG, per_device) + array.shape[1:])
    return shaped[:, first_row:first_row + number].reshape((N_SEG * number,) + array.shape[1:])


def couple_level(coefficients, skeleton, partner_list, inverse_len):
    padded_coefs = jnp.pad(coefficients, ((4, 4), (0, 0), (0, 0)))
    padded_skel = jnp.pad(skeleton, ((4, 4), (0, 0), (0, 0)))

    def one_box(index):
        chosen = index + 4 + partner_list[index]
        kernel = settle(kernel_tiles(skeleton[index][None], padded_skel[chosen], inverse_len))
        return jnp.einsum("mij,mjp->ip", widen(kernel), widen(padded_coefs[chosen]), precision=lax.Precision.HIGHEST)

    return lax.map(one_box, jnp.arange(coefficients.shape[0], dtype=jnp.int32))


def reference(points, vectors, lengthscale, leaf_basis, local_transfer, upper_transfer, local_skeleton, upper_skeleton, near_offsets, local_coupling, upper_coupling):
    inverse_len = 1.0 / lengthscale
    leaves = LEAF_DEV * N_SEG
    leaf_levels = LEAF_DEV.bit_length() - 1
    seg_levels = N_SEG.bit_length() - 1
    top_level = leaf_levels + seg_levels - 2
    point_blocks = points.reshape(DIM, leaves, LEAF).transpose(1, 0, 2)
    vector_blocks = vectors.reshape(PROBES, leaves, LEAF).transpose(1, 0, 2)
    padded_points = jnp.pad(point_blocks, ((REACH, REACH), (0, 0), (0, 0)))
    padded_vectors = jnp.pad(vector_blocks, ((REACH, REACH), (0, 0), (0, 0)))

    def near_leaf(index):
        chosen = index + REACH + near_offsets[index]
        kernel = settle(kernel_tiles(point_blocks[index][None], padded_points[chosen], inverse_len))
        return jnp.einsum("mij,mpj->pi", widen(kernel), widen(padded_vectors[chosen]), precision=lax.Precision.HIGHEST)

    near_part = lax.map(near_leaf, jnp.arange(leaves, dtype=jnp.int32))
    coefficients = [settle(jnp.einsum("trl,tpl->trp", widen(leaf_basis), widen(vector_blocks), precision=lax.Precision.HIGHEST))]
    transfers = []
    skeletons = []
    partner_lists = []
    for height in range(top_level + 1):
        if height <= leaf_levels:
            boxes = LEAF_DEV >> height
            first_row = 2 * LEAF_DEV - 2 * boxes
            skeletons.append(level_rows(local_skeleton, 2 * LEAF_DEV - 1, first_row, boxes))
            partner_lists.append(level_rows(local_coupling, 2 * LEAF_DEV - 1, first_row, boxes))
        else:
            above = height - leaf_levels
            first_row = N_SEG - (N_SEG >> (above - 1))
            number = N_SEG >> above
            skeletons.append(upper_skeleton[first_row:first_row + number])
            partner_lists.append(upper_coupling[first_row:first_row + number])
        if height < top_level:
            if height < leaf_levels:
                boxes = LEAF_DEV >> height
                first_row = 2 * LEAF_DEV - 2 * boxes
                transfer = level_rows(local_transfer, 2 * LEAF_DEV - 2, first_row, boxes)
            else:
                above = height - leaf_levels
                first_row = 2 * N_SEG - 2 * (N_SEG >> above)
                transfer = upper_transfer[first_row:first_row + (N_SEG >> above)]
            transfers.append(transfer)
            terms = jnp.einsum("trs,trp->tsp", widen(transfer), widen(coefficients[-1]), precision=lax.Precision.HIGHEST)
            paired = terms.reshape((terms.shape[0] // 2, 2) + terms.shape[1:])
            coefficients.append(settle(paired[:, 0] + paired[:, 1]))
    couplings = [couple_level(coefficients[height], skeletons[height], partner_lists[height], inverse_len) for height in range(top_level + 1)]
    field = couplings[top_level]
    for height in range(top_level - 1, -1, -1):
        spread = jnp.repeat(widen(settle(field)), 2, axis=0)
        field = couplings[height] + jnp.einsum("trs,tsp->trp", widen(transfers[height]), spread, precision=lax.Precision.HIGHEST)
    far_part = jnp.einsum("trl,trp->tpl", widen(leaf_basis), widen(settle(field)), precision=lax.Precision.HIGHEST)
    summed = near_part + far_part
    return summed.transpose(1, 0, 2).reshape(PROBES, leaves * LEAF)
```

```python
import functools

import jax
import jax.numpy as jnp
from jax import lax
from jax.experimental import pallas as pl
from jax.experimental.pallas import tpu as pltpu
from jax.sharding import PartitionSpec as P

REACH = 8


FAR_OFFSETS = (-4, -3, -2, 2, 3, 4)


LOG2E = 1.4426950408889634


def split3(x):
    a = x.astype(jnp.bfloat16); r = x - a.astype(jnp.float32)
    b = r.astype(jnp.bfloat16); r = r - b.astype(jnp.float32)
    return a, b, r.astype(jnp.bfloat16)


def augment(points, inv):
    s = (points.astype(jnp.float32) * inv).astype(jnp.bfloat16)
    w = s.astype(jnp.float32)
    t1, t2, t3 = split3(w * LOG2E)
    n = (-0.5 * LOG2E) * jnp.sum(w * w, axis=-2, keepdims=True)
    n1, n2, n3 = (x.astype(jnp.float32) for x in split3(n))
    row = lax.broadcasted_iota(jnp.int32, w.shape, w.ndim - 2)
    nr = jnp.where(row % 3 == 0, n1, jnp.where(row % 3 == 1, n2, n3))
    src_n = jnp.where(row < 3, nr, jnp.where(row < 6, 1.0, 0.0)).astype(jnp.bfloat16)
    tgt_n = jnp.where(row < 3, 1.0, jnp.where(row < 6, nr, 0.0)).astype(jnp.bfloat16)
    return (jnp.concatenate([s, s, s, src_n], axis=-2), jnp.concatenate([t1, t2, t3, tgt_n], axis=-2))


def near_kernel(reach, leaf, dims, off_ref, inv_ref, wide_ref, out_ref, src, tgt):
    leaf_dev, near = off_ref.shape
    rows = wide_ref.shape[0]
    inv = inv_ref[...]
    blocks = wide_ref.shape[1] // leaf

    def prep(b, _):
        col = pl.ds(pl.multiple_of(b * leaf, leaf), leaf)
        s, t = augment(wide_ref[0:dims, col], inv)
        src[col, :] = s.T
        tgt[:, col] = t
        return 0

    lax.fori_loop(0, blocks, prep, 0)

    def one(t, _):
        own = pl.ds(pl.multiple_of((t + reach) * leaf, leaf), leaf)
        acc = None
        target = tgt[:, own]
        for m in range(near):
            c = t + reach + off_ref[t, m]
            col = pl.ds(pl.multiple_of(c * leaf, leaf), leaf)
            k = jnp.exp2(jnp.dot(src[col, :], target, preferred_element_type=jnp.float32))
            d = jnp.dot(wide_ref[dims:rows, col], k.astype(jnp.bfloat16), preferred_element_type=jnp.float32)
            acc = d if acc is None else acc + d
        out_ref[:, pl.ds(pl.multiple_of(t * leaf, leaf), leaf)] = acc
        return 0

    lax.fori_loop(0, leaf_dev, one, 0)


def near_product(offsets, inverse_len, widened, leaf, dims):
    leaf_dev = offsets.shape[0]
    width = widened.shape[1]
    depth = 4 * dims
    return pl.pallas_call(
        functools.partial(near_kernel, REACH, leaf, dims),
        in_specs=[pl.BlockSpec(memory_space=pltpu.SMEM)] + [pl.BlockSpec(memory_space=pltpu.VMEM)] * 2,
        out_specs=pl.BlockSpec(memory_space=pltpu.VMEM),
        out_shape=jax.ShapeDtypeStruct((widened.shape[0] - dims, leaf_dev * leaf), jnp.float32),
        scratch_shapes=[pltpu.VMEM((width, depth), jnp.bfloat16), pltpu.VMEM((depth, width), jnp.bfloat16)],
        compiler_params=pltpu.CompilerParams(vmem_limit_bytes=40 << 20),
    )(offsets, inverse_len[:, None], widened)


def with_halo(cells, sides, width):
    for axis, dim in sides:
        count = lax.axis_size(axis)
        ends = count - 1
        head = lax.slice_in_dim(cells, 0, width, axis=dim)
        tail = lax.slice_in_dim(cells, cells.shape[dim] - width, cells.shape[dim], axis=dim)
        cells = jnp.concatenate(
            [
                lax.ppermute(tail, axis, [(i, (i + 1) % count) for i in range(ends)]),
                cells,
                lax.ppermute(head, axis, [((i + 1) % count, i) for i in range(ends)]),
            ],
            axis=dim,
        )
    return cells


def passed_along(x, axis, by):
    peers = lax.axis_size(axis)
    pairs = [(i, i + by) for i in range(peers) if 0 <= i + by < peers]
    return lax.ppermute(x, axis, pairs)


def kernel_tiles(targets, sources, inverse_len):
    target_scaled = (targets.astype(jnp.float32) * inverse_len[:, None]).astype(jnp.bfloat16)
    source_scaled = (sources.astype(jnp.float32) * inverse_len[:, None]).astype(jnp.bfloat16)
    target_wide = target_scaled.astype(jnp.float32)
    source_wide = source_scaled.astype(jnp.float32)
    target_norm = jnp.sum(target_wide * target_wide, axis=-2)
    source_norm = jnp.sum(source_wide * source_wide, axis=-2)
    inner = jnp.einsum(
        "...dm,...dk->...mk", target_scaled, source_scaled, preferred_element_type=jnp.float32
    )
    return jnp.exp(-0.5 * (target_norm[..., :, None] + source_norm[..., None, :] - 2.0 * inner))


def pick_row(array, position):
    return lax.dynamic_index_in_dim(array, position, 0, keepdims=False)


def body(
    points,
    vectors,
    lengthscale,
    leaf_basis,
    local_transfer,
    upper_transfer,
    local_skeleton,
    upper_skeleton,
    near_offsets,
    local_coupling,
    upper_coupling,
):
    inverse_len = 1.0 / lengthscale
    dims = points.shape[0]
    probes = vectors.shape[0]
    leaf_dev, rank_size, leaf_size = leaf_basis.shape
    leaf_levels = leaf_dev.bit_length() - 1
    segments = lax.axis_size("seg")
    seg_levels = segments.bit_length() - 1
    top_cross = seg_levels - 2
    device = lax.axis_index("seg")
    stacked = jnp.concatenate([points, vectors], axis=0)
    widened = with_halo(stacked, (("seg", 1),), REACH * leaf_size)
    near_part = near_product(near_offsets, inverse_len, widened, leaf_size, dims)
    vector_blocks = vectors.reshape(probes, leaf_dev, leaf_size)
    level_coefs = [
        jnp.einsum(
            "trl,ptl->trp", leaf_basis, vector_blocks, preferred_element_type=jnp.float32
        ).astype(jnp.bfloat16)
    ]
    for height in range(leaf_levels):
        boxes = leaf_dev >> height
        first_row = 2 * leaf_dev - 2 * boxes
        transfer = local_transfer[first_row : first_row + boxes]
        terms = jnp.einsum(
            "trs,trp->tsp", transfer, level_coefs[-1], preferred_element_type=jnp.float32
        )
        paired = terms.reshape(boxes // 2, 2, rank_size, probes)
        level_coefs.append((paired[:, 0] + paired[:, 1]).astype(jnp.bfloat16))
    local_fields = []
    for height in range(leaf_levels + 1):
        boxes = leaf_dev >> height
        first_row = 2 * leaf_dev - 2 * boxes
        skeleton = local_skeleton[first_row : first_row + boxes]
        partner_list = local_coupling[first_row : first_row + boxes]
        packed = jnp.concatenate(
            [level_coefs[height].reshape(boxes, -1), skeleton.reshape(boxes, -1)], axis=1
        )
        reach_devices = -(-4 // boxes)
        moves = [m for m in range(reach_devices, -reach_devices - 1, -1) if m != 0]
        arrived = dict(((m, passed_along(packed, "seg", m)) for m in moves))
        ordered = (
            [arrived[m] for m in range(reach_devices, 0, -1)]
            + [packed]
            + [arrived[-m] for m in range(1, reach_devices + 1)]
        )
        rows_all = jnp.concatenate(ordered, axis=0)
        base = reach_devices * boxes
        coef_all = rows_all[:, : rank_size * probes].reshape(-1, rank_size, probes)
        skel_all = rows_all[:, rank_size * probes :].reshape(-1, dims, rank_size)
        field = jnp.zeros((boxes, rank_size, probes), jnp.float32)
        for offset in FAR_OFFSETS:
            partner_coefs = coef_all[base + offset : base + offset + boxes]
            partner_skel = skel_all[base + offset : base + offset + boxes]
            kernel = kernel_tiles(skeleton, partner_skel, inverse_len).astype(jnp.bfloat16)
            product = jnp.einsum(
                "tij,tjp->tip", kernel, partner_coefs, preferred_element_type=jnp.float32
            )
            weight = jnp.sum((partner_list == offset).astype(jnp.float32), axis=1)
            field = field + weight[:, None, None] * product
        local_fields.append(field)
    cross_coefs = [level_coefs[leaf_levels][0]]
    roots = lax.all_gather(level_coefs[leaf_levels], "seg", axis=0, tiled=True)
    every_level = [roots]
    for above in range(top_cross):
        boxes = segments >> above
        first_row = 2 * segments - 2 * boxes
        transfer = upper_transfer[first_row : first_row + boxes]
        terms = jnp.einsum(
            "trs,trp->tsp", transfer, every_level[-1], preferred_element_type=jnp.float32
        )
        paired = terms.reshape(boxes // 2, 2, rank_size, probes)
        every_level.append((paired[:, 0] + paired[:, 1]).astype(jnp.bfloat16))
    for above in range(1, top_cross + 1):
        cross_coefs.append(pick_row(every_level[above], device // (1 << above)))
    cross_fields = {}
    for above in range(1, top_cross + 1):
        position = device // (1 << above)
        first_row = segments - (segments >> above - 1)
        skeleton = pick_row(upper_skeleton, first_row + position)
        partner_list = pick_row(upper_coupling, first_row + position)
        padded_level = jnp.pad(every_level[above], ((4, 4), (0, 0), (0, 0)))
        field = jnp.zeros((rank_size, probes), jnp.float32)
        for offset in FAR_OFFSETS:
            if abs(offset) * (1 << above) < segments:
                partner_coefs = pick_row(padded_level, position + 4 + offset)
                partner_skel = pick_row(upper_skeleton, first_row + position + offset)
                kernel = kernel_tiles(skeleton, partner_skel, inverse_len).astype(jnp.bfloat16)
                product = jnp.dot(kernel, partner_coefs, preferred_element_type=jnp.float32)
                weight = jnp.sum((partner_list == offset).astype(jnp.float32))
                field = field + weight * product
        cross_fields[above] = field
    field = cross_fields[top_cross]
    for above in range(top_cross, 0, -1):
        child = above - 1
        position = device // (1 << child)
        first_row = 2 * segments - 2 * (segments >> child)
        transfer = pick_row(upper_transfer, first_row + position)
        spread = jnp.dot(transfer, field.astype(jnp.bfloat16), preferred_element_type=jnp.float32)
        if child > 0:
            field = cross_fields[child] + spread
        else:
            field = local_fields[leaf_levels][0] + spread
    level_field = field[None]
    for height in range(leaf_levels - 1, -1, -1):
        boxes = leaf_dev >> height
        first_row = 2 * leaf_dev - 2 * boxes
        transfer = local_transfer[first_row : first_row + boxes]
        spread = jnp.repeat(level_field.astype(jnp.bfloat16), 2, axis=0)
        level_field = local_fields[height] + jnp.einsum(
            "trs,tsp->trp", transfer, spread, preferred_element_type=jnp.float32
        )
    far_part = jnp.einsum(
        "trl,trp->tpl",
        leaf_basis,
        level_field.astype(jnp.bfloat16),
        preferred_element_type=jnp.float32,
    )
    return near_part + far_part.transpose(1, 0, 2).reshape(probes, leaf_dev * leaf_size)


def solution(mesh):
    in_specs = (
        P(None, ("groups", "seg")),
        P(None, ("groups", "seg")),
        P("groups"),
        P(("groups", "seg"), None, None),
        P(("groups", "seg"), None, None),
        P("groups", None, None),
        P(("groups", "seg"), None, None),
        P("groups", None, None),
        P(("groups", "seg"), None),
        P(("groups", "seg"), None),
        P("groups", None),
    )
    out_specs = P(None, ("groups", "seg"))
    return jax.shard_map(body, mesh=mesh, in_specs=in_specs, out_specs=out_specs, check_vma=False)
```

```python
import functools

import jax
import jax.numpy as jnp
from jax import lax
from jax.experimental import pallas as pl
from jax.experimental.pallas import tpu as pltpu
from jax.sharding import PartitionSpec as P

REACH = 8
CPL_REACH = 4

LOG2E = 1.4426950408889634


def split3(x):
    a = x.astype(jnp.bfloat16); r = x - a.astype(jnp.float32)
    b = r.astype(jnp.bfloat16); r = r - b.astype(jnp.float32)
    return a, b, r.astype(jnp.bfloat16)


def augment(points, inv):
    s = (points.astype(jnp.float32) * inv).astype(jnp.bfloat16)
    w = s.astype(jnp.float32)
    t1, t2, t3 = split3(w * LOG2E)
    n = (-0.5 * LOG2E) * jnp.sum(w * w, axis=-2, keepdims=True)
    n1, n2, n3 = (x.astype(jnp.float32) for x in split3(n))
    row = lax.broadcasted_iota(jnp.int32, w.shape, w.ndim - 2)
    nr = jnp.where(row % 3 == 0, n1, jnp.where(row % 3 == 1, n2, n3))
    src_n = jnp.where(row < 3, nr, jnp.where(row < 6, 1.0, 0.0)).astype(jnp.bfloat16)
    tgt_n = jnp.where(row < 3, 1.0, jnp.where(row < 6, nr, 0.0)).astype(jnp.bfloat16)
    return (jnp.concatenate([s, s, s, src_n], axis=-2), jnp.concatenate([t1, t2, t3, tgt_n], axis=-2))


NN = (((1,), (0,)), ((), ()))
NT = (((1,), (1,)), ((), ()))


def mul(a, b, dims=NN):
    return lax.dot_general(a, b, dims, preferred_element_type=jnp.float32)


def first_box(leaf_dev, height):
    return 2 * leaf_dev - 2 * (leaf_dev >> height)


def upward_kernel(basis_ref, vectors_ref, transfer_ref, skeleton_ref, own, head, tail, top):
    leaf_dev, _, leaf = basis_ref.shape
    probes = vectors_ref.shape[0]
    levels = leaf_dev.bit_length()
    own[:, probes:, :] = skeleton_ref[...]
    coefs = []
    for t in range(leaf_dev):
        c = mul(vectors_ref[:, t * leaf : (t + 1) * leaf], basis_ref[t], NT)
        coefs.append(c.astype(jnp.bfloat16))
        own[t, 0:probes, :] = coefs[-1]
    for height in range(levels - 1):
        row = first_box(leaf_dev, height)
        above = first_box(leaf_dev, height + 1)
        terms = [mul(c, transfer_ref[row + b]) for b, c in enumerate(coefs)]
        coefs = [(terms[2 * b] + terms[2 * b + 1]).astype(jnp.bfloat16) for b in range(len(terms) // 2)]
        for b, c in enumerate(coefs):
            own[above + b, 0:probes, :] = c
    near_rows = 0
    for height in range(levels):
        boxes = leaf_dev >> height
        row = first_box(leaf_dev, height)
        if boxes >= CPL_REACH:
            head[near_rows : near_rows + CPL_REACH] = own[row : row + CPL_REACH]
            tail[near_rows : near_rows + CPL_REACH] = own[row + boxes - CPL_REACH : row + boxes]
            near_rows += CPL_REACH
        else:
            top[...] = own[row:]
            break


def vmem(count):
    return [pl.BlockSpec(memory_space=pltpu.VMEM)] * count


def upward(leaf_basis, vectors, transfer, skeleton):
    leaf_dev, rank, _ = leaf_basis.shape
    rows = vectors.shape[0] + skeleton.shape[1]
    edge = sum(CPL_REACH for h in range(leaf_dev.bit_length()) if leaf_dev >> h >= CPL_REACH)
    high = sum(leaf_dev >> h for h in range(leaf_dev.bit_length()) if leaf_dev >> h < CPL_REACH)
    shapes = [(n, rows, rank) for n in (skeleton.shape[0], edge, edge, high)]
    return pl.pallas_call(
        upward_kernel,
        in_specs=vmem(4),
        out_specs=vmem(4),
        out_shape=[jax.ShapeDtypeStruct(s, jnp.bfloat16) for s in shapes],
        cost_estimate=pl.CostEstimate(flops=4 * 10**9, bytes_accessed=4 << 20, transcendentals=0),
        compiler_params=pltpu.CompilerParams(vmem_limit_bytes=24 << 20),
    )(leaf_basis, vectors, transfer, skeleton)


def near_kernel(off_ref, inv_ref, left_ref, points_ref, vectors_ref, right_ref, out_ref, src, tgt, vec):
    leaf_dev, near = off_ref.shape
    dims = points_ref.shape[0]
    rows = left_ref.shape[0]
    leaf = points_ref.shape[1] // leaf_dev
    inv = inv_ref[...]

    def part(b):
        return pl.ds(pl.multiple_of(b * leaf, leaf), leaf)

    def side(ref, at):
        def step(b, _):
            s, _t = augment(ref[0:dims, part(b)], inv)
            src[part(at + b), :] = s.T
            vec[:, part(at + b)] = ref[dims:rows, part(b)]
            return 0

        lax.fori_loop(0, REACH, step, 0)

    def middle(b, _):
        s, t = augment(points_ref[:, part(b)], inv)
        src[part(REACH + b), :] = s.T
        tgt[:, part(b)] = t
        vec[:, part(REACH + b)] = vectors_ref[:, part(b)]
        return 0

    side(left_ref, 0)
    lax.fori_loop(0, leaf_dev, middle, 0)
    side(right_ref, REACH + leaf_dev)

    def one(t, _):
        acc = None
        target = tgt[:, part(t)]
        for m in range(near):
            col = part(t + REACH + off_ref[t, m])
            k = jnp.exp2(mul(src[col, :], target)).astype(jnp.bfloat16)
            d = mul(vec[:, col], k)
            acc = d if acc is None else acc + d
        out_ref[:, part(t)] = acc
        return 0

    lax.fori_loop(0, leaf_dev, one, 0)


def near_product(offsets, inverse, left, points, vectors, right):
    dims, count = points.shape
    probes = vectors.shape[0]
    width = count + left.shape[1] + right.shape[1]
    depth = 4 * dims
    return pl.pallas_call(
        near_kernel,
        in_specs=[pl.BlockSpec(memory_space=pltpu.SMEM)] + vmem(5),
        out_specs=pl.BlockSpec(memory_space=pltpu.VMEM),
        out_shape=jax.ShapeDtypeStruct((probes, count), jnp.float32),
        scratch_shapes=[
            pltpu.VMEM((width, depth), jnp.bfloat16),
            pltpu.VMEM((depth, count), jnp.bfloat16),
            pltpu.VMEM((probes, width), jnp.bfloat16),
        ],
        cost_estimate=pl.CostEstimate(flops=40 * 10**9, bytes_accessed=4 << 20, transcendentals=33 << 20),
        compiler_params=pltpu.CompilerParams(vmem_limit_bytes=32 << 20),
    )(offsets, inverse, left, points, vectors, right)


def far_kernel(
    seg_count, place_ref, local_ref, upper_ref, inv_ref, basis_ref, transfer_ref, up_transfer_ref, up_skeleton_ref,
    own_ref, left_ref, right_ref, top_ref, near_ref, out_ref, win, high, src, tgt,
):
    leaf_dev, rank, leaf = basis_ref.shape
    probes = near_ref.shape[0]
    levels = leaf_dev.bit_length()
    cross = seg_count.bit_length() - 3
    pad = CPL_REACH
    place = place_ref[0]
    high[...] = jnp.zeros_like(high)
    at = 0
    edge = 0
    store = 0
    offset = 0
    starts = []
    for height in range(levels):
        boxes = leaf_dev >> height
        row = first_box(leaf_dev, height)
        starts.append(at)
        if boxes >= pad:
            win[at : at + pad] = left_ref[edge : edge + pad]
            win[at + pad : at + pad + boxes] = own_ref[row : row + boxes]
            win[at + pad + boxes : at + 2 * pad + boxes] = right_ref[edge : edge + pad]
            edge += pad
        else:
            for g in range(seg_count):
                spot = store + pad + g * boxes
                high[spot : spot + boxes] = top_ref[g, offset : offset + boxes]
            win[at : at + 2 * pad + boxes] = high[pl.ds(store + place * boxes, 2 * pad + boxes)]
            offset += boxes
            if height < levels - 1:
                store += 2 * pad + boxes * seg_count
        at += 2 * pad + boxes
    for above in range(1, cross + 1):
        boxes = seg_count >> above
        row = 2 * seg_count - 4 * boxes
        skel_row = seg_count - 2 * boxes
        below = store + pad
        store += 2 * pad + 2 * boxes
        for b in range(boxes):
            c = mul(high[below + 2 * b, 0:probes, :], up_transfer_ref[row + 2 * b]) + mul(
                high[below + 2 * b + 1, 0:probes, :], up_transfer_ref[row + 2 * b + 1]
            )
            high[store + pad + b, 0:probes, :] = c.astype(jnp.bfloat16)
            high[store + pad + b, probes:, :] = up_skeleton_ref[skel_row + b]
        starts.append(at)
        win[at : at + 2 * pad + 1] = high[pl.ds(store + place // (1 << above), 2 * pad + 1)]
        at += 2 * pad + 1
    inv = inv_ref[...]
    for r in range(at):
        s, t = augment(win[r, probes:, :], inv)
        src[r * rank : (r + 1) * rank, :] = s.T
        tgt[r] = t

    def coupled(base, list_ref, row):
        picks = [base + list_ref[row, m] for m in range(list_ref.shape[1])]
        stacked = jnp.concatenate([src[pl.ds(pl.multiple_of(p * rank, rank), rank), :] for p in picks], axis=0)
        k = jnp.exp2(mul(stacked, tgt[base])).astype(jnp.bfloat16)
        total = None
        for m, p in enumerate(picks):
            d = mul(win[p, 0:probes, :], k[m * rank : (m + 1) * rank])
            total = d if total is None else total + d
        return total

    field = None
    for above in range(cross, 0, -1):
        boxes = seg_count >> above
        position = place // (1 << above)
        own = coupled(starts[levels - 1 + above] + pad, upper_ref, seg_count - 2 * boxes + position)
        if field is not None:
            own = own + mul(field, up_transfer_ref[2 * seg_count - 2 * boxes + position], NT)
        field = own.astype(jnp.bfloat16)
    spread = mul(field, up_transfer_ref[place], NT)
    fields = None
    for height in range(levels - 1, -1, -1):
        boxes = leaf_dev >> height
        row = first_box(leaf_dev, height)
        now = []
        for b in range(boxes):
            own = coupled(starts[height] + pad + b, local_ref, row + b)
            if fields is None:
                own = own + spread
            else:
                own = own + mul(fields[b // 2], transfer_ref[row + b], NT)
            now.append(own.astype(jnp.bfloat16))
        fields = now
    for t in range(leaf_dev):
        cols = slice(t * leaf, (t + 1) * leaf)
        out_ref[:, cols] = near_ref[:, cols] + mul(fields[t], basis_ref[t])


def far_sum(
    seg_count, place, local_coupling, upper_coupling, inverse, leaf_basis, local_transfer, upper_transfer,
    upper_skeleton, own, left, right, top, near_part,
):
    leaf_dev, rank, _ = leaf_basis.shape
    rows = own.shape[1]
    dims = upper_skeleton.shape[1]
    pad = 2 * CPL_REACH
    counts = [leaf_dev >> h for h in range(leaf_dev.bit_length())]
    uppers = [seg_count >> a for a in range(1, seg_count.bit_length() - 2)]
    window = sum(n + pad for n in counts) + len(uppers) * (pad + 1)
    high = sum(n * seg_count + pad for n in counts if n < CPL_REACH) + sum(n + pad for n in uppers)
    return pl.pallas_call(
        functools.partial(far_kernel, seg_count),
        in_specs=[pl.BlockSpec(memory_space=pltpu.SMEM)] * 3 + vmem(10),
        out_specs=pl.BlockSpec(memory_space=pltpu.VMEM),
        out_shape=jax.ShapeDtypeStruct(near_part.shape, jnp.float32),
        scratch_shapes=[
            pltpu.VMEM((window, rows, rank), jnp.bfloat16),
            pltpu.VMEM((high, rows, rank), jnp.bfloat16),
            pltpu.VMEM((window * rank, 4 * dims), jnp.bfloat16),
            pltpu.VMEM((window, 4 * dims, rank), jnp.bfloat16),
        ],
        cost_estimate=pl.CostEstimate(flops=10**10, bytes_accessed=6 << 20, transcendentals=1 << 20),
        compiler_params=pltpu.CompilerParams(vmem_limit_bytes=40 << 20),
    )(
        place, local_coupling, upper_coupling, inverse, leaf_basis, local_transfer, upper_transfer, upper_skeleton,
        own, left, right, top, near_part,
    )


def body(
    points,
    vectors,
    lengthscale,
    leaf_basis,
    local_transfer,
    upper_transfer,
    local_skeleton,
    upper_skeleton,
    near_offsets,
    local_coupling,
    upper_coupling,
):
    inverse = (1.0 / lengthscale)[:, None]
    leaf = leaf_basis.shape[2]
    count = points.shape[1]
    seg_count = lax.axis_size("seg")
    place = lax.axis_index("seg").astype(jnp.int32)[None]
    ahead = [(i, i + 1) for i in range(seg_count - 1)]
    back = [(i + 1, i) for i in range(seg_count - 1)]
    reach = REACH * leaf
    first = jnp.concatenate([points[:, :reach], vectors[:, :reach]], axis=0)
    last = jnp.concatenate([points[:, count - reach :], vectors[:, count - reach :]], axis=0)
    left = lax.ppermute(last, "seg", ahead)
    right = lax.ppermute(first, "seg", back)
    own, head, tail, top = upward(leaf_basis, vectors, local_transfer, local_skeleton)
    far_left = lax.ppermute(tail, "seg", ahead)
    far_right = lax.ppermute(head, "seg", back)
    far_top = lax.all_gather(top, "seg", axis=0, tiled=False)
    near_part = near_product(near_offsets, inverse, left, points, vectors, right)
    return far_sum(
        seg_count, place, local_coupling, upper_coupling, inverse, leaf_basis, local_transfer, upper_transfer,
        upper_skeleton, own, far_left, far_right, far_top, near_part,
    )


def solution(mesh):
    in_specs = (
        P(None, ("groups", "seg")),
        P(None, ("groups", "seg")),
        P("groups"),
        P(("groups", "seg"), None, None),
        P(("groups", "seg"), None, None),
        P("groups", None, None),
        P(("groups", "seg"), None, None),
        P("groups", None, None),
        P(("groups", "seg"), None),
        P(("groups", "seg"), None),
        P("groups", None),
    )
    out_specs = P(None, ("groups", "seg"))
    return jax.shard_map(body, mesh=mesh, in_specs=in_specs, out_specs=out_specs, check_vma=False)
```

```python
import functools

import jax
import jax.numpy as jnp
from jax import lax
from jax.experimental import pallas as pl
from jax.experimental.pallas import tpu as pltpu
from jax.sharding import PartitionSpec as P

REACH = 8
CPL_REACH = 4

LOG2E = 1.4426950408889634


def split3(x):
    a = x.astype(jnp.bfloat16); r = x - a.astype(jnp.float32)
    b = r.astype(jnp.bfloat16); r = r - b.astype(jnp.float32)
    return a, b, r.astype(jnp.bfloat16)


def augment(points, inv):
    s = (points.astype(jnp.float32) * inv).astype(jnp.bfloat16)
    w = s.astype(jnp.float32)
    t1, t2, t3 = split3(w * LOG2E)
    n = (-0.5 * LOG2E) * jnp.sum(w * w, axis=-2, keepdims=True)
    n1, n2, n3 = (x.astype(jnp.float32) for x in split3(n))
    row = lax.broadcasted_iota(jnp.int32, w.shape, w.ndim - 2)
    nr = jnp.where(row % 3 == 0, n1, jnp.where(row % 3 == 1, n2, n3))
    src_n = jnp.where(row < 3, nr, jnp.where(row < 6, 1.0, 0.0)).astype(jnp.bfloat16)
    tgt_n = jnp.where(row < 3, 1.0, jnp.where(row < 6, nr, 0.0)).astype(jnp.bfloat16)
    return (jnp.concatenate([s, s, s, src_n], axis=-2), jnp.concatenate([t1, t2, t3, tgt_n], axis=-2))


NN = (((1,), (0,)), ((), ()))
NT = (((1,), (1,)), ((), ()))


def mul(a, b, dims=NN):
    return lax.dot_general(a, b, dims, preferred_element_type=jnp.float32)


def first_box(leaf_dev, height):
    return 2 * leaf_dev - 2 * (leaf_dev >> height)


MESH = pl.DeviceIdType.MESH


def upward_kernel(
    seg_count, basis_ref, points_ref, vectors_ref, transfer_ref, skeleton_ref,
    own, left_p, left_v, right_p, right_v, far_left, far_right, far_top,
    head, tail, top, send, recv, top_send, top_recv,
):
    me = lax.axis_index("seg")
    reach = left_p.shape[1]
    count = points_ref.shape[1]
    barrier = pltpu.get_barrier_semaphore()

    def greet(d, _):
        pl.semaphore_signal(barrier, inc=1, device_id={"seg": lax.rem(me + d, seg_count)}, device_id_type=MESH)
        return 0

    lax.fori_loop(1, seg_count, greet, 0)
    pl.semaphore_wait(barrier, seg_count - 1)

    def link(k, source, target, peer):
        return pltpu.make_async_remote_copy(
            src_ref=source, dst_ref=target, send_sem=send.at[k], recv_sem=recv.at[k],
            device_id={"seg": peer}, device_id_type=MESH,
        )

    end = pl.ds(count - reach, reach)
    ahead = lambda: [
        link(0, points_ref.at[:, end], left_p, me + 1),
        link(1, vectors_ref.at[:, end], left_v, me + 1),
    ]
    back = lambda: [
        link(2, points_ref.at[:, pl.ds(0, reach)], right_p, me - 1),
        link(3, vectors_ref.at[:, pl.ds(0, reach)], right_v, me - 1),
    ]
    far_ahead = lambda: [link(4, tail, far_left, me + 1)]
    far_back = lambda: [link(5, head, far_right, me - 1)]

    def spread(d):
        return pltpu.make_async_remote_copy(
            src_ref=top, dst_ref=far_top.at[me], send_sem=top_send.at[d], recv_sem=top_recv.at[d],
            device_id={"seg": lax.rem(me + d, seg_count)}, device_id_type=MESH,
        )

    @pl.when(me < seg_count - 1)
    def _():
        for copy in ahead():
            copy.start()

    @pl.when(me > 0)
    def _():
        for copy in back():
            copy.start()

    leaf_dev, _, leaf = basis_ref.shape
    probes = vectors_ref.shape[0]
    levels = leaf_dev.bit_length()
    own[:, probes:, :] = skeleton_ref[...]
    coefs = []
    for t in range(leaf_dev):
        c = mul(vectors_ref[:, t * leaf : (t + 1) * leaf], basis_ref[t], NT)
        coefs.append(c.astype(jnp.bfloat16))
        own[t, 0:probes, :] = coefs[-1]
    for height in range(levels - 1):
        row = first_box(leaf_dev, height)
        above = first_box(leaf_dev, height + 1)
        terms = [mul(c, transfer_ref[row + b]) for b, c in enumerate(coefs)]
        coefs = [(terms[2 * b] + terms[2 * b + 1]).astype(jnp.bfloat16) for b in range(len(terms) // 2)]
        for b, c in enumerate(coefs):
            own[above + b, 0:probes, :] = c
    near_rows = 0
    for height in range(levels):
        boxes = leaf_dev >> height
        row = first_box(leaf_dev, height)
        if boxes >= CPL_REACH:
            head[near_rows : near_rows + CPL_REACH] = own[row : row + CPL_REACH]
            tail[near_rows : near_rows + CPL_REACH] = own[row + boxes - CPL_REACH : row + boxes]
            near_rows += CPL_REACH
        else:
            top[...] = own[row:]
            break
    far_top[me] = top[...]

    def start(d, _):
        spread(d).start()
        return 0

    lax.fori_loop(1, seg_count, start, 0)

    @pl.when(me < seg_count - 1)
    def _():
        far_ahead()[0].start()

    @pl.when(me > 0)
    def _():
        far_back()[0].start()

    @pl.when(me < seg_count - 1)
    def _():
        for copy in ahead() + far_ahead():
            copy.wait_send()
        for copy in back() + far_back():
            copy.wait_recv()

    @pl.when(me > 0)
    def _():
        for copy in back() + far_back():
            copy.wait_send()
        for copy in ahead() + far_ahead():
            copy.wait_recv()

    @pl.when(me == 0)
    def _():
        for ref in (left_p, left_v, far_left):
            ref[...] = jnp.zeros_like(ref)

    @pl.when(me == seg_count - 1)
    def _():
        for ref in (right_p, right_v, far_right):
            ref[...] = jnp.zeros_like(ref)

    def finish(d, _):
        spread(d).wait()
        return 0

    lax.fori_loop(1, seg_count, finish, 0)


def vmem(count):
    return [pl.BlockSpec(memory_space=pltpu.VMEM)] * count


def upward(seg_count, leaf_basis, points, vectors, transfer, skeleton):
    leaf_dev, rank, leaf = leaf_basis.shape
    dims, probes = points.shape[0], vectors.shape[0]
    rows = probes + dims
    reach = REACH * leaf
    edge = sum(CPL_REACH for h in range(leaf_dev.bit_length()) if leaf_dev >> h >= CPL_REACH)
    high = sum(leaf_dev >> h for h in range(leaf_dev.bit_length()) if leaf_dev >> h < CPL_REACH)
    shapes = [
        (skeleton.shape[0], rows, rank), (dims, reach), (probes, reach), (dims, reach), (probes, reach),
        (edge, rows, rank), (edge, rows, rank), (seg_count, high, rows, rank),
    ]
    return pl.pallas_call(
        functools.partial(upward_kernel, seg_count),
        in_specs=vmem(5),
        out_specs=vmem(8),
        out_shape=[jax.ShapeDtypeStruct(s, jnp.bfloat16) for s in shapes],
        scratch_shapes=[
            pltpu.VMEM((edge, rows, rank), jnp.bfloat16),
            pltpu.VMEM((edge, rows, rank), jnp.bfloat16),
            pltpu.VMEM((high, rows, rank), jnp.bfloat16),
            pltpu.SemaphoreType.DMA((6,)),
            pltpu.SemaphoreType.DMA((6,)),
            pltpu.SemaphoreType.DMA((seg_count,)),
            pltpu.SemaphoreType.DMA((seg_count,)),
        ],
        cost_estimate=pl.CostEstimate(flops=4 * 10**9, bytes_accessed=4 << 20, transcendentals=0),
        compiler_params=pltpu.CompilerParams(vmem_limit_bytes=24 << 20, collective_id=0, has_side_effects=True),
    )(leaf_basis, points, vectors, transfer, skeleton)


def near_kernel(
    off_ref, inv_ref, left_p, left_v, points_ref, vectors_ref, right_p, right_v, out_ref, src, tgt, vec
):
    leaf_dev, near = off_ref.shape
    leaf = points_ref.shape[1] // leaf_dev
    inv = inv_ref[...]

    def part(b):
        return pl.ds(pl.multiple_of(b * leaf, leaf), leaf)

    def side(pts, vcs, at):
        def step(b, _):
            s, _t = augment(pts[:, part(b)], inv)
            src[part(at + b), :] = s.T
            vec[:, part(at + b)] = vcs[:, part(b)]
            return 0

        lax.fori_loop(0, REACH, step, 0)

    def middle(b, _):
        s, t = augment(points_ref[:, part(b)], inv)
        src[part(REACH + b), :] = s.T
        tgt[:, part(b)] = t
        vec[:, part(REACH + b)] = vectors_ref[:, part(b)]
        return 0

    side(left_p, left_v, 0)
    lax.fori_loop(0, leaf_dev, middle, 0)
    side(right_p, right_v, REACH + leaf_dev)

    def one(t, _):
        acc = None
        target = tgt[:, part(t)]
        for m in range(near):
            col = part(t + REACH + off_ref[t, m])
            k = jnp.exp2(mul(src[col, :], target)).astype(jnp.bfloat16)
            d = mul(vec[:, col], k)
            acc = d if acc is None else acc + d
        out_ref[:, part(t)] = acc
        return 0

    lax.fori_loop(0, leaf_dev, one, 0)


def near_product(offsets, inverse, left_p, left_v, points, vectors, right_p, right_v):
    dims, count = points.shape
    probes = vectors.shape[0]
    width = count + left_p.shape[1] + right_p.shape[1]
    depth = 4 * dims
    return pl.pallas_call(
        near_kernel,
        in_specs=[pl.BlockSpec(memory_space=pltpu.SMEM)] + vmem(7),
        out_specs=pl.BlockSpec(memory_space=pltpu.VMEM),
        out_shape=jax.ShapeDtypeStruct((probes, count), jnp.float32),
        scratch_shapes=[
            pltpu.VMEM((width, depth), jnp.bfloat16),
            pltpu.VMEM((depth, count), jnp.bfloat16),
            pltpu.VMEM((probes, width), jnp.bfloat16),
        ],
        cost_estimate=pl.CostEstimate(flops=40 * 10**9, bytes_accessed=4 << 20, transcendentals=33 << 20),
        compiler_params=pltpu.CompilerParams(vmem_limit_bytes=32 << 20),
    )(offsets, inverse, left_p, left_v, points, vectors, right_p, right_v)


def far_kernel(
    seg_count, place_ref, local_ref, upper_ref, inv_ref, basis_ref, transfer_ref, up_transfer_ref, up_skeleton_ref,
    own_ref, left_ref, right_ref, top_ref, near_ref, out_ref, win, high, src, tgt,
):
    leaf_dev, rank, leaf = basis_ref.shape
    probes = near_ref.shape[0]
    levels = leaf_dev.bit_length()
    cross = seg_count.bit_length() - 3
    pad = CPL_REACH
    place = place_ref[0]
    high[...] = jnp.zeros_like(high)
    at = 0
    edge = 0
    store = 0
    offset = 0
    starts = []
    for height in range(levels):
        boxes = leaf_dev >> height
        row = first_box(leaf_dev, height)
        starts.append(at)
        if boxes >= pad:
            win[at : at + pad] = left_ref[edge : edge + pad]
            win[at + pad : at + pad + boxes] = own_ref[row : row + boxes]
            win[at + pad + boxes : at + 2 * pad + boxes] = right_ref[edge : edge + pad]
            edge += pad
        else:
            for g in range(seg_count):
                spot = store + pad + g * boxes
                high[spot : spot + boxes] = top_ref[g, offset : offset + boxes]
            win[at : at + 2 * pad + boxes] = high[pl.ds(store + place * boxes, 2 * pad + boxes)]
            offset += boxes
            if height < levels - 1:
                store += 2 * pad + boxes * seg_count
        at += 2 * pad + boxes
    for above in range(1, cross + 1):
        boxes = seg_count >> above
        row = 2 * seg_count - 4 * boxes
        skel_row = seg_count - 2 * boxes
        below = store + pad
        store += 2 * pad + 2 * boxes
        for b in range(boxes):
            c = mul(high[below + 2 * b, 0:probes, :], up_transfer_ref[row + 2 * b]) + mul(
                high[below + 2 * b + 1, 0:probes, :], up_transfer_ref[row + 2 * b + 1]
            )
            high[store + pad + b, 0:probes, :] = c.astype(jnp.bfloat16)
            high[store + pad + b, probes:, :] = up_skeleton_ref[skel_row + b]
        starts.append(at)
        win[at : at + 2 * pad + 1] = high[pl.ds(store + place // (1 << above), 2 * pad + 1)]
        at += 2 * pad + 1
    inv = inv_ref[...]
    for r in range(at):
        s, t = augment(win[r, probes:, :], inv)
        src[r * rank : (r + 1) * rank, :] = s.T
        tgt[r] = t

    def coupled(base, list_ref, row):
        picks = [base + list_ref[row, m] for m in range(list_ref.shape[1])]
        stacked = jnp.concatenate([src[pl.ds(pl.multiple_of(p * rank, rank), rank), :] for p in picks], axis=0)
        k = jnp.exp2(mul(stacked, tgt[base])).astype(jnp.bfloat16)
        total = None
        for m, p in enumerate(picks):
            d = mul(win[p, 0:probes, :], k[m * rank : (m + 1) * rank])
            total = d if total is None else total + d
        return total

    field = None
    for above in range(cross, 0, -1):
        boxes = seg_count >> above
        position = place // (1 << above)
        own = coupled(starts[levels - 1 + above] + pad, upper_ref, seg_count - 2 * boxes + position)
        if field is not None:
            own = own + mul(field, up_transfer_ref[2 * seg_count - 2 * boxes + position], NT)
        field = own.astype(jnp.bfloat16)
    spread = mul(field, up_transfer_ref[place], NT)
    fields = None
    for height in range(levels - 1, -1, -1):
        boxes = leaf_dev >> height
        row = first_box(leaf_dev, height)
        now = []
        for b in range(boxes):
            own = coupled(starts[height] + pad + b, local_ref, row + b)
            if fields is None:
                own = own + spread
            else:
                own = own + mul(fields[b // 2], transfer_ref[row + b], NT)
            now.append(own.astype(jnp.bfloat16))
        fields = now
    for t in range(leaf_dev):
        cols = slice(t * leaf, (t + 1) * leaf)
        out_ref[:, cols] = near_ref[:, cols] + mul(fields[t], basis_ref[t])


def far_sum(
    seg_count, place, local_coupling, upper_coupling, inverse, leaf_basis, local_transfer, upper_transfer,
    upper_skeleton, own, left, right, top, near_part,
):
    leaf_dev, rank, _ = leaf_basis.shape
    rows = own.shape[1]
    dims = upper_skeleton.shape[1]
    pad = 2 * CPL_REACH
    counts = [leaf_dev >> h for h in range(leaf_dev.bit_length())]
    uppers = [seg_count >> a for a in range(1, seg_count.bit_length() - 2)]
    window = sum(n + pad for n in counts) + len(uppers) * (pad + 1)
    high = sum(n * seg_count + pad for n in counts if n < CPL_REACH) + sum(n + pad for n in uppers)
    return pl.pallas_call(
        functools.partial(far_kernel, seg_count),
        in_specs=[pl.BlockSpec(memory_space=pltpu.SMEM)] * 3 + vmem(10),
        out_specs=pl.BlockSpec(memory_space=pltpu.VMEM),
        out_shape=jax.ShapeDtypeStruct(near_part.shape, jnp.float32),
        scratch_shapes=[
            pltpu.VMEM((window, rows, rank), jnp.bfloat16),
            pltpu.VMEM((high, rows, rank), jnp.bfloat16),
            pltpu.VMEM((window * rank, 4 * dims), jnp.bfloat16),
            pltpu.VMEM((window, 4 * dims, rank), jnp.bfloat16),
        ],
        cost_estimate=pl.CostEstimate(flops=10**10, bytes_accessed=6 << 20, transcendentals=1 << 20),
        compiler_params=pltpu.CompilerParams(vmem_limit_bytes=40 << 20),
    )(
        place, local_coupling, upper_coupling, inverse, leaf_basis, local_transfer, upper_transfer, upper_skeleton,
        own, left, right, top, near_part,
    )


def body(
    points,
    vectors,
    lengthscale,
    leaf_basis,
    local_transfer,
    upper_transfer,
    local_skeleton,
    upper_skeleton,
    near_offsets,
    local_coupling,
    upper_coupling,
):
    inverse = (1.0 / lengthscale)[:, None]
    seg_count = lax.axis_size("seg")
    place = lax.axis_index("seg").astype(jnp.int32)[None]
    own, left_p, left_v, right_p, right_v, far_left, far_right, far_top = upward(
        seg_count, leaf_basis, points, vectors, local_transfer, local_skeleton
    )
    near_part = near_product(near_offsets, inverse, left_p, left_v, points, vectors, right_p, right_v)
    return far_sum(
        seg_count, place, local_coupling, upper_coupling, inverse, leaf_basis, local_transfer, upper_transfer,
        upper_skeleton, own, far_left, far_right, far_top, near_part,
    )


def solution(mesh):
    in_specs = (
        P(None, ("groups", "seg")),
        P(None, ("groups", "seg")),
        P("groups"),
        P(("groups", "seg"), None, None),
        P(("groups", "seg"), None, None),
        P("groups", None, None),
        P(("groups", "seg"), None, None),
        P("groups", None, None),
        P(("groups", "seg"), None),
        P(("groups", "seg"), None),
        P("groups", None),
    )
    out_specs = P(None, ("groups", "seg"))
    return jax.shard_map(body, mesh=mesh, in_specs=in_specs, out_specs=out_specs, check_vma=False)
```

```python
import functools

import jax
import jax.numpy as jnp
from jax import lax
from jax.experimental import pallas as pl
from jax.experimental.pallas import tpu as pltpu
from jax.sharding import PartitionSpec as P

REACH = 8
CPL_REACH = 4

LOG2E = 1.4426950408889634


def split3(x):
    a = x.astype(jnp.bfloat16); r = x - a.astype(jnp.float32)
    b = r.astype(jnp.bfloat16); r = r - b.astype(jnp.float32)
    return a, b, r.astype(jnp.bfloat16)


def augment(points, inv):
    s = (points.astype(jnp.float32) * inv).astype(jnp.bfloat16)
    w = s.astype(jnp.float32)
    t1, t2, t3 = split3(w * LOG2E)
    n = (-0.5 * LOG2E) * jnp.sum(w * w, axis=-2, keepdims=True)
    n1, n2, n3 = (x.astype(jnp.float32) for x in split3(n))
    row = lax.broadcasted_iota(jnp.int32, w.shape, w.ndim - 2)
    nr = jnp.where(row % 3 == 0, n1, jnp.where(row % 3 == 1, n2, n3))
    src_n = jnp.where(row < 3, nr, jnp.where(row < 6, 1.0, 0.0)).astype(jnp.bfloat16)
    tgt_n = jnp.where(row < 3, 1.0, jnp.where(row < 6, nr, 0.0)).astype(jnp.bfloat16)
    return (jnp.concatenate([s, s, s, src_n], axis=-2), jnp.concatenate([t1, t2, t3, tgt_n], axis=-2))


NN = (((1,), (0,)), ((), ()))
NT = (((1,), (1,)), ((), ()))


def mul(a, b, dims=NN):
    return lax.dot_general(a, b, dims, preferred_element_type=jnp.float32)


def first_box(leaf_dev, height):
    return 2 * leaf_dev - 2 * (leaf_dev >> height)


MESH = pl.DeviceIdType.MESH


def upward_kernel(
    seg_count, basis_ref, points_ref, vectors_ref, transfer_ref, skeleton_ref,
    own, left_p, left_v, right_p, right_v, far_left, far_right, far_top, far_root,
    head, tail, top, root, send, recv, top_send, top_recv, root_send, root_recv,
):
    me = lax.axis_index("seg")
    reach = left_p.shape[1]
    count = points_ref.shape[1]
    barrier = pltpu.get_barrier_semaphore()

    def greet(d, _):
        pl.semaphore_signal(barrier, inc=1, device_id={"seg": lax.rem(me + d, seg_count)}, device_id_type=MESH)
        return 0

    lax.fori_loop(1, seg_count, greet, 0)
    pl.semaphore_wait(barrier, seg_count - 1)

    def link(k, source, target, peer):
        return pltpu.make_async_remote_copy(
            src_ref=source, dst_ref=target, send_sem=send.at[k], recv_sem=recv.at[k],
            device_id={"seg": peer}, device_id_type=MESH,
        )

    end = pl.ds(count - reach, reach)
    ahead = lambda: [
        link(0, points_ref.at[:, end], left_p, me + 1),
        link(1, vectors_ref.at[:, end], left_v, me + 1),
    ]
    back = lambda: [
        link(2, points_ref.at[:, pl.ds(0, reach)], right_p, me - 1),
        link(3, vectors_ref.at[:, pl.ds(0, reach)], right_v, me - 1),
    ]
    far_ahead = lambda: [link(4, tail, far_left, me + 1)]
    far_back = lambda: [link(5, head, far_right, me - 1)]

    def spread(d):
        return pltpu.make_async_remote_copy(
            src_ref=root, dst_ref=far_root.at[me], send_sem=root_send.at[d], recv_sem=root_recv.at[d],
            device_id={"seg": lax.rem(me + d, seg_count)}, device_id_type=MESH,
        )

    def nearby(k, by):
        return pltpu.make_async_remote_copy(
            src_ref=top, dst_ref=far_top.at[me], send_sem=top_send.at[k], recv_sem=top_recv.at[k],
            device_id={"seg": me + by}, device_id_type=MESH,
        )

    steps = list(enumerate([by for by in range(-CPL_REACH, CPL_REACH + 1) if by != 0]))

    def inside(by):
        return me + by < seg_count if by > 0 else me + by >= 0

    @pl.when(me < seg_count - 1)
    def _():
        for copy in ahead():
            copy.start()

    @pl.when(me > 0)
    def _():
        for copy in back():
            copy.start()

    leaf_dev, _, leaf = basis_ref.shape
    probes = vectors_ref.shape[0]
    levels = leaf_dev.bit_length()
    own[:, probes:, :] = skeleton_ref[...]
    coefs = []
    for t in range(leaf_dev):
        c = mul(vectors_ref[:, t * leaf : (t + 1) * leaf], basis_ref[t], NT)
        coefs.append(c.astype(jnp.bfloat16))
        own[t, 0:probes, :] = coefs[-1]
    for height in range(levels - 1):
        row = first_box(leaf_dev, height)
        above = first_box(leaf_dev, height + 1)
        terms = [mul(c, transfer_ref[row + b]) for b, c in enumerate(coefs)]
        coefs = [(terms[2 * b] + terms[2 * b + 1]).astype(jnp.bfloat16) for b in range(len(terms) // 2)]
        for b, c in enumerate(coefs):
            own[above + b, 0:probes, :] = c
    near_rows = 0
    for height in range(levels):
        boxes = leaf_dev >> height
        row = first_box(leaf_dev, height)
        if boxes >= CPL_REACH:
            head[near_rows : near_rows + CPL_REACH] = own[row : row + CPL_REACH]
            tail[near_rows : near_rows + CPL_REACH] = own[row + boxes - CPL_REACH : row + boxes]
            near_rows += CPL_REACH
        else:
            top[...] = own[row:]
            break
    far_top[me] = top[...]
    root[...] = coefs[0]
    far_root[me] = coefs[0]
    for k, by in steps:

        @pl.when(inside(by))
        def _():
            nearby(k, by).start()


    def start(d, _):
        spread(d).start()
        return 0

    lax.fori_loop(1, seg_count, start, 0)

    @pl.when(me < seg_count - 1)
    def _():
        far_ahead()[0].start()

    @pl.when(me > 0)
    def _():
        far_back()[0].start()

    @pl.when(me < seg_count - 1)
    def _():
        for copy in ahead() + far_ahead():
            copy.wait_send()
        for copy in back() + far_back():
            copy.wait_recv()

    @pl.when(me > 0)
    def _():
        for copy in back() + far_back():
            copy.wait_send()
        for copy in ahead() + far_ahead():
            copy.wait_recv()

    @pl.when(me == 0)
    def _():
        for ref in (left_p, left_v, far_left):
            ref[...] = jnp.zeros_like(ref)

    @pl.when(me == seg_count - 1)
    def _():
        for ref in (right_p, right_v, far_right):
            ref[...] = jnp.zeros_like(ref)

    def finish(d, _):
        spread(d).wait()
        return 0

    lax.fori_loop(1, seg_count, finish, 0)
    for k, by in steps:

        @pl.when(inside(by))
        def _():
            nearby(k, by).wait_send()

        @pl.when(inside(-by))
        def _():
            nearby(k, by).wait_recv()


def vmem(count):
    return [pl.BlockSpec(memory_space=pltpu.VMEM)] * count


def upward(seg_count, leaf_basis, points, vectors, transfer, skeleton):
    leaf_dev, rank, leaf = leaf_basis.shape
    dims, probes = points.shape[0], vectors.shape[0]
    rows = probes + dims
    reach = REACH * leaf
    edge = sum(CPL_REACH for h in range(leaf_dev.bit_length()) if leaf_dev >> h >= CPL_REACH)
    high = sum(leaf_dev >> h for h in range(leaf_dev.bit_length()) if leaf_dev >> h < CPL_REACH)
    shapes = [
        (skeleton.shape[0], rows, rank), (dims, reach), (probes, reach), (dims, reach), (probes, reach),
        (edge, rows, rank), (edge, rows, rank), (seg_count, high, rows, rank), (seg_count, probes, rank),
    ]
    return pl.pallas_call(
        functools.partial(upward_kernel, seg_count),
        in_specs=vmem(5),
        out_specs=vmem(9),
        out_shape=[jax.ShapeDtypeStruct(s, jnp.bfloat16) for s in shapes],
        scratch_shapes=[
            pltpu.VMEM((edge, rows, rank), jnp.bfloat16),
            pltpu.VMEM((edge, rows, rank), jnp.bfloat16),
            pltpu.VMEM((high, rows, rank), jnp.bfloat16),
            pltpu.VMEM((probes, rank), jnp.bfloat16),
            pltpu.SemaphoreType.DMA((6,)),
            pltpu.SemaphoreType.DMA((6,)),
            pltpu.SemaphoreType.DMA((2 * CPL_REACH,)),
            pltpu.SemaphoreType.DMA((2 * CPL_REACH,)),
            pltpu.SemaphoreType.DMA((seg_count,)),
            pltpu.SemaphoreType.DMA((seg_count,)),
        ],
        cost_estimate=pl.CostEstimate(flops=4 * 10**9, bytes_accessed=4 << 20, transcendentals=0),
        compiler_params=pltpu.CompilerParams(vmem_limit_bytes=24 << 20, collective_id=0, has_side_effects=True),
    )(leaf_basis, points, vectors, transfer, skeleton)


def near_kernel(
    off_ref, inv_ref, left_p, left_v, points_ref, vectors_ref, right_p, right_v, out_ref, src, tgt, vec
):
    leaf_dev, near = off_ref.shape
    leaf = points_ref.shape[1] // leaf_dev
    inv = inv_ref[...]

    def part(b):
        return pl.ds(pl.multiple_of(b * leaf, leaf), leaf)

    def side(pts, vcs, at):
        def step(b, _):
            s, _t = augment(pts[:, part(b)], inv)
            src[part(at + b), :] = s.T
            vec[:, part(at + b)] = vcs[:, part(b)]
            return 0

        lax.fori_loop(0, REACH, step, 0)

    def middle(b, _):
        s, t = augment(points_ref[:, part(b)], inv)
        src[part(REACH + b), :] = s.T
        tgt[:, part(b)] = t
        vec[:, part(REACH + b)] = vectors_ref[:, part(b)]
        return 0

    side(left_p, left_v, 0)
    lax.fori_loop(0, leaf_dev, middle, 0)
    side(right_p, right_v, REACH + leaf_dev)

    def one(t, _):
        acc = None
        target = tgt[:, part(t)]
        for m in range(near):
            col = part(t + REACH + off_ref[t, m])
            k = jnp.exp2(mul(src[col, :], target)).astype(jnp.bfloat16)
            d = mul(vec[:, col], k)
            acc = d if acc is None else acc + d
        out_ref[:, part(t)] = acc
        return 0

    lax.fori_loop(0, leaf_dev, one, 0)


def near_product(offsets, inverse, left_p, left_v, points, vectors, right_p, right_v):
    dims, count = points.shape
    probes = vectors.shape[0]
    width = count + left_p.shape[1] + right_p.shape[1]
    depth = 4 * dims
    return pl.pallas_call(
        near_kernel,
        in_specs=[pl.BlockSpec(memory_space=pltpu.SMEM)] + vmem(7),
        out_specs=pl.BlockSpec(memory_space=pltpu.VMEM),
        out_shape=jax.ShapeDtypeStruct((probes, count), jnp.float32),
        scratch_shapes=[
            pltpu.VMEM((width, depth), jnp.bfloat16),
            pltpu.VMEM((depth, count), jnp.bfloat16),
            pltpu.VMEM((probes, width), jnp.bfloat16),
        ],
        cost_estimate=pl.CostEstimate(flops=40 * 10**9, bytes_accessed=4 << 20, transcendentals=33 << 20),
        compiler_params=pltpu.CompilerParams(vmem_limit_bytes=32 << 20),
    )(offsets, inverse, left_p, left_v, points, vectors, right_p, right_v)


def far_kernel(
    seg_count, place_ref, local_ref, upper_ref, inv_ref, basis_ref, transfer_ref, up_transfer_ref, up_skeleton_ref,
    own_ref, left_ref, right_ref, top_ref, root_ref, near_ref, out_ref, win, high, src, tgt,
):
    leaf_dev, rank, leaf = basis_ref.shape
    probes = near_ref.shape[0]
    levels = leaf_dev.bit_length()
    cross = seg_count.bit_length() - 3
    pad = CPL_REACH
    place = place_ref[0]
    high[...] = jnp.zeros_like(high)
    at = 0
    edge = 0
    store = 0
    offset = 0
    starts = []
    for height in range(levels):
        boxes = leaf_dev >> height
        row = first_box(leaf_dev, height)
        starts.append(at)
        if boxes >= pad:
            win[at : at + pad] = left_ref[edge : edge + pad]
            win[at + pad : at + pad + boxes] = own_ref[row : row + boxes]
            win[at + pad + boxes : at + 2 * pad + boxes] = right_ref[edge : edge + pad]
            edge += pad
        else:
            for g in range(seg_count):
                spot = store + pad + g * boxes
                high[spot : spot + boxes] = top_ref[g, offset : offset + boxes]
            win[at : at + 2 * pad + boxes] = high[pl.ds(store + place * boxes, 2 * pad + boxes)]
            offset += boxes
            if height < levels - 1:
                store += 2 * pad + boxes * seg_count
        at += 2 * pad + boxes
    for above in range(1, cross + 1):
        boxes = seg_count >> above
        row = 2 * seg_count - 4 * boxes
        skel_row = seg_count - 2 * boxes
        below = store + pad
        store += 2 * pad + 2 * boxes
        for b in range(boxes):
            pair = [root_ref[i] if above == 1 else high[below + i, 0:probes, :] for i in (2 * b, 2 * b + 1)]
            c = mul(pair[0], up_transfer_ref[row + 2 * b]) + mul(pair[1], up_transfer_ref[row + 2 * b + 1])
            high[store + pad + b, 0:probes, :] = c.astype(jnp.bfloat16)
            high[store + pad + b, probes:, :] = up_skeleton_ref[skel_row + b]
        starts.append(at)
        win[at : at + 2 * pad + 1] = high[pl.ds(store + place // (1 << above), 2 * pad + 1)]
        at += 2 * pad + 1
    inv = inv_ref[...]
    for r in range(at):
        s, t = augment(win[r, probes:, :], inv)
        src[r * rank : (r + 1) * rank, :] = s.T
        tgt[r] = t

    def coupled(base, list_ref, row):
        picks = [base + list_ref[row, m] for m in range(list_ref.shape[1])]
        stacked = jnp.concatenate([src[pl.ds(pl.multiple_of(p * rank, rank), rank), :] for p in picks], axis=0)
        k = jnp.exp2(mul(stacked, tgt[base])).astype(jnp.bfloat16)
        total = None
        for m, p in enumerate(picks):
            d = mul(win[p, 0:probes, :], k[m * rank : (m + 1) * rank])
            total = d if total is None else total + d
        return total

    field = None
    for above in range(cross, 0, -1):
        boxes = seg_count >> above
        position = place // (1 << above)
        own = coupled(starts[levels - 1 + above] + pad, upper_ref, seg_count - 2 * boxes + position)
        if field is not None:
            own = own + mul(field, up_transfer_ref[2 * seg_count - 2 * boxes + position], NT)
        field = own.astype(jnp.bfloat16)
    spread = mul(field, up_transfer_ref[place], NT)
    fields = None
    for height in range(levels - 1, -1, -1):
        boxes = leaf_dev >> height
        row = first_box(leaf_dev, height)
        now = []
        for b in range(boxes):
            own = coupled(starts[height] + pad + b, local_ref, row + b)
            if fields is None:
                own = own + spread
            else:
                own = own + mul(fields[b // 2], transfer_ref[row + b], NT)
            now.append(own.astype(jnp.bfloat16))
        fields = now
    for t in range(leaf_dev):
        cols = slice(t * leaf, (t + 1) * leaf)
        out_ref[:, cols] = near_ref[:, cols] + mul(fields[t], basis_ref[t])


def far_sum(
    seg_count, place, local_coupling, upper_coupling, inverse, leaf_basis, local_transfer, upper_transfer,
    upper_skeleton, own, left, right, top, root, near_part,
):
    leaf_dev, rank, _ = leaf_basis.shape
    rows = own.shape[1]
    dims = upper_skeleton.shape[1]
    pad = 2 * CPL_REACH
    counts = [leaf_dev >> h for h in range(leaf_dev.bit_length())]
    uppers = [seg_count >> a for a in range(1, seg_count.bit_length() - 2)]
    window = sum(n + pad for n in counts) + len(uppers) * (pad + 1)
    high = sum(n * seg_count + pad for n in counts if n < CPL_REACH) + sum(n + pad for n in uppers)
    return pl.pallas_call(
        functools.partial(far_kernel, seg_count),
        in_specs=[pl.BlockSpec(memory_space=pltpu.SMEM)] * 3 + vmem(11),
        out_specs=pl.BlockSpec(memory_space=pltpu.VMEM),
        out_shape=jax.ShapeDtypeStruct(near_part.shape, jnp.float32),
        scratch_shapes=[
            pltpu.VMEM((window, rows, rank), jnp.bfloat16),
            pltpu.VMEM((high, rows, rank), jnp.bfloat16),
            pltpu.VMEM((window * rank, 4 * dims), jnp.bfloat16),
            pltpu.VMEM((window, 4 * dims, rank), jnp.bfloat16),
        ],
        cost_estimate=pl.CostEstimate(flops=10**10, bytes_accessed=6 << 20, transcendentals=1 << 20),
        compiler_params=pltpu.CompilerParams(vmem_limit_bytes=40 << 20),
    )(
        place, local_coupling, upper_coupling, inverse, leaf_basis, local_transfer, upper_transfer, upper_skeleton,
        own, left, right, top, root, near_part,
    )


def body(
    points,
    vectors,
    lengthscale,
    leaf_basis,
    local_transfer,
    upper_transfer,
    local_skeleton,
    upper_skeleton,
    near_offsets,
    local_coupling,
    upper_coupling,
):
    inverse = (1.0 / lengthscale)[:, None]
    seg_count = lax.axis_size("seg")
    place = lax.axis_index("seg").astype(jnp.int32)[None]
    own, left_p, left_v, right_p, right_v, far_left, far_right, far_top, far_root = upward(
        seg_count, leaf_basis, points, vectors, local_transfer, local_skeleton
    )
    near_part = near_product(near_offsets, inverse, left_p, left_v, points, vectors, right_p, right_v)
    return far_sum(
        seg_count, place, local_coupling, upper_coupling, inverse, leaf_basis, local_transfer, upper_transfer,
        upper_skeleton, own, far_left, far_right, far_top, far_root, near_part,
    )


def solution(mesh):
    in_specs = (
        P(None, ("groups", "seg")),
        P(None, ("groups", "seg")),
        P("groups"),
        P(("groups", "seg"), None, None),
        P(("groups", "seg"), None, None),
        P("groups", None, None),
        P(("groups", "seg"), None, None),
        P("groups", None, None),
        P(("groups", "seg"), None),
        P(("groups", "seg"), None),
        P("groups", None),
    )
    out_specs = P(None, ("groups", "seg"))
    return jax.shard_map(body, mesh=mesh, in_specs=in_specs, out_specs=out_specs, check_vma=False)
```

```python
import functools

import jax
import jax.numpy as jnp
from jax import lax
from jax.experimental import pallas as pl
from jax.experimental.pallas import tpu as pltpu
from jax.sharding import PartitionSpec as P

REACH = 8
CPL_REACH = 4

LOG2E = 1.4426950408889634


def split3(x):
    a = x.astype(jnp.bfloat16); r = x - a.astype(jnp.float32)
    b = r.astype(jnp.bfloat16); r = r - b.astype(jnp.float32)
    return a, b, r.astype(jnp.bfloat16)


def augment(points, inv):
    s = (points.astype(jnp.float32) * inv).astype(jnp.bfloat16)
    w = s.astype(jnp.float32)
    t1, t2, t3 = split3(w * LOG2E)
    n = (-0.5 * LOG2E) * jnp.sum(w * w, axis=-2, keepdims=True)
    n1, n2, n3 = (x.astype(jnp.float32) for x in split3(n))
    row = lax.broadcasted_iota(jnp.int32, w.shape, w.ndim - 2)
    nr = jnp.where(row % 3 == 0, n1, jnp.where(row % 3 == 1, n2, n3))
    src_n = jnp.where(row < 3, nr, jnp.where(row < 6, 1.0, 0.0)).astype(jnp.bfloat16)
    tgt_n = jnp.where(row < 3, 1.0, jnp.where(row < 6, nr, 0.0)).astype(jnp.bfloat16)
    return (jnp.concatenate([s, s, s, src_n], axis=-2), jnp.concatenate([t1, t2, t3, tgt_n], axis=-2))


NN = (((1,), (0,)), ((), ()))
NT = (((1,), (1,)), ((), ()))


def mul(a, b, dims=NN):
    return lax.dot_general(a, b, dims, preferred_element_type=jnp.float32)


def first_box(leaf_dev, height):
    return 2 * leaf_dev - 2 * (leaf_dev >> height)


MESH = pl.DeviceIdType.MESH


def upward_kernel(
    seg_count, basis_ref, points_ref, vectors_ref, transfer_ref, skeleton_ref,
    own, left_p, left_v, right_p, right_v, far_left, far_right, far_top, far_root,
    head, tail, top, root, send, recv, top_send, top_recv, root_send, root_recv,
):
    me = lax.axis_index("seg")
    reach = left_p.shape[1]
    count = points_ref.shape[1]
    barrier = pltpu.get_barrier_semaphore()

    def greet(d, _):
        pl.semaphore_signal(barrier, inc=1, device_id={"seg": lax.rem(me + d, seg_count)}, device_id_type=MESH)
        return 0

    lax.fori_loop(1, seg_count, greet, 0)
    pl.semaphore_wait(barrier, seg_count - 1)

    def link(k, source, target, peer):
        return pltpu.make_async_remote_copy(
            src_ref=source, dst_ref=target, send_sem=send.at[k], recv_sem=recv.at[k],
            device_id={"seg": peer}, device_id_type=MESH,
        )

    end = pl.ds(count - reach, reach)
    ahead = lambda: [
        link(0, points_ref.at[:, end], left_p, me + 1),
        link(1, vectors_ref.at[:, end], left_v, me + 1),
    ]
    back = lambda: [
        link(2, points_ref.at[:, pl.ds(0, reach)], right_p, me - 1),
        link(3, vectors_ref.at[:, pl.ds(0, reach)], right_v, me - 1),
    ]
    far_ahead = lambda: [link(4, tail, far_left, me + 1)]
    far_back = lambda: [link(5, head, far_right, me - 1)]

    def spread(d):
        return pltpu.make_async_remote_copy(
            src_ref=root, dst_ref=far_root.at[me], send_sem=root_send.at[d], recv_sem=root_recv.at[d],
            device_id={"seg": lax.rem(me + d, seg_count)}, device_id_type=MESH,
        )

    def nearby(k, by):
        return pltpu.make_async_remote_copy(
            src_ref=top, dst_ref=far_top.at[me], send_sem=top_send.at[k], recv_sem=top_recv.at[k],
            device_id={"seg": me + by}, device_id_type=MESH,
        )

    steps = list(enumerate([by for by in range(-CPL_REACH, CPL_REACH + 1) if by != 0]))

    def inside(by):
        return me + by < seg_count if by > 0 else me + by >= 0

    @pl.when(me < seg_count - 1)
    def _():
        for copy in ahead():
            copy.start()

    @pl.when(me > 0)
    def _():
        for copy in back():
            copy.start()

    leaf_dev, _, leaf = basis_ref.shape
    probes = vectors_ref.shape[0]
    levels = leaf_dev.bit_length()
    own[:, probes:, :] = skeleton_ref[...]
    coefs = []
    for t in range(leaf_dev):
        c = mul(vectors_ref[:, t * leaf : (t + 1) * leaf], basis_ref[t], NT)
        coefs.append(c.astype(jnp.bfloat16))
        own[t, 0:probes, :] = coefs[-1]
    for height in range(levels - 1):
        row = first_box(leaf_dev, height)
        above = first_box(leaf_dev, height + 1)
        terms = [mul(c, transfer_ref[row + b]) for b, c in enumerate(coefs)]
        coefs = [(terms[2 * b] + terms[2 * b + 1]).astype(jnp.bfloat16) for b in range(len(terms) // 2)]
        for b, c in enumerate(coefs):
            own[above + b, 0:probes, :] = c
    near_rows = 0
    for height in range(levels):
        boxes = leaf_dev >> height
        row = first_box(leaf_dev, height)
        if boxes >= CPL_REACH:
            head[near_rows : near_rows + CPL_REACH] = own[row : row + CPL_REACH]
            tail[near_rows : near_rows + CPL_REACH] = own[row + boxes - CPL_REACH : row + boxes]
            near_rows += CPL_REACH
        else:
            top[...] = own[row:]
            break
    far_top[me] = top[...]
    root[...] = coefs[0]
    far_root[me] = coefs[0]
    for k, by in steps:

        @pl.when(inside(by))
        def _():
            nearby(k, by).start()


    def start(d, _):
        spread(d).start()
        return 0

    lax.fori_loop(1, seg_count, start, 0)

    @pl.when(me < seg_count - 1)
    def _():
        far_ahead()[0].start()

    @pl.when(me > 0)
    def _():
        far_back()[0].start()

    @pl.when(me < seg_count - 1)
    def _():
        for copy in ahead() + far_ahead():
            copy.wait_send()
        for copy in back() + far_back():
            copy.wait_recv()

    @pl.when(me > 0)
    def _():
        for copy in back() + far_back():
            copy.wait_send()
        for copy in ahead() + far_ahead():
            copy.wait_recv()

    @pl.when(me == 0)
    def _():
        for ref in (left_p, left_v, far_left):
            ref[...] = jnp.zeros_like(ref)

    @pl.when(me == seg_count - 1)
    def _():
        for ref in (right_p, right_v, far_right):
            ref[...] = jnp.zeros_like(ref)

    def finish(d, _):
        spread(d).wait()
        return 0

    lax.fori_loop(1, seg_count, finish, 0)
    for k, by in steps:

        @pl.when(inside(by))
        def _():
            nearby(k, by).wait_send()

        @pl.when(inside(-by))
        def _():
            nearby(k, by).wait_recv()


def vmem(count):
    return [pl.BlockSpec(memory_space=pltpu.VMEM)] * count


def upward(seg_count, leaf_basis, points, vectors, transfer, skeleton):
    leaf_dev, rank, leaf = leaf_basis.shape
    dims, probes = points.shape[0], vectors.shape[0]
    rows = probes + dims
    reach = REACH * leaf
    edge = sum(CPL_REACH for h in range(leaf_dev.bit_length()) if leaf_dev >> h >= CPL_REACH)
    high = sum(leaf_dev >> h for h in range(leaf_dev.bit_length()) if leaf_dev >> h < CPL_REACH)
    shapes = [
        (skeleton.shape[0], rows, rank), (dims, reach), (probes, reach), (dims, reach), (probes, reach),
        (edge, rows, rank), (edge, rows, rank), (seg_count, high, rows, rank), (seg_count, probes, rank),
    ]
    return pl.pallas_call(
        functools.partial(upward_kernel, seg_count),
        in_specs=vmem(5),
        out_specs=vmem(9),
        out_shape=[jax.ShapeDtypeStruct(s, jnp.bfloat16) for s in shapes],
        scratch_shapes=[
            pltpu.VMEM((edge, rows, rank), jnp.bfloat16),
            pltpu.VMEM((edge, rows, rank), jnp.bfloat16),
            pltpu.VMEM((high, rows, rank), jnp.bfloat16),
            pltpu.VMEM((probes, rank), jnp.bfloat16),
            pltpu.SemaphoreType.DMA((6,)),
            pltpu.SemaphoreType.DMA((6,)),
            pltpu.SemaphoreType.DMA((2 * CPL_REACH,)),
            pltpu.SemaphoreType.DMA((2 * CPL_REACH,)),
            pltpu.SemaphoreType.DMA((seg_count,)),
            pltpu.SemaphoreType.DMA((seg_count,)),
        ],
        cost_estimate=pl.CostEstimate(flops=4 * 10**9, bytes_accessed=4 << 20, transcendentals=0),
        compiler_params=pltpu.CompilerParams(vmem_limit_bytes=24 << 20, collective_id=0, has_side_effects=True),
    )(leaf_basis, points, vectors, transfer, skeleton)


def near_kernel(
    off_ref, inv_ref, left_p, left_v, points_ref, vectors_ref, right_p, right_v, out_ref, src, tgt, vec
):
    leaf_dev, near = off_ref.shape
    leaf = points_ref.shape[1] // leaf_dev
    inv = inv_ref[...]

    def part(b):
        return pl.ds(pl.multiple_of(b * leaf, leaf), leaf)

    def side(pts, vcs, at):
        def step(b, _):
            s, _t = augment(pts[:, part(b)], inv)
            src[part(at + b), :] = s.T
            vec[:, part(at + b)] = vcs[:, part(b)]
            return 0

        lax.fori_loop(0, REACH, step, 0)

    def middle(b, _):
        s, t = augment(points_ref[:, part(b)], inv)
        src[part(REACH + b), :] = s.T
        tgt[:, part(b)] = t
        vec[:, part(REACH + b)] = vectors_ref[:, part(b)]
        return 0

    side(left_p, left_v, 0)
    lax.fori_loop(0, leaf_dev, middle, 0)
    side(right_p, right_v, REACH + leaf_dev)

    def one(t, _):
        acc = None
        target = tgt[:, part(t)]
        for m in range(0, near, 2):
            cols = [part(t + REACH + off_ref[t, n]) for n in range(m, min(m + 2, near))]
            source = jnp.concatenate([src[col, :] for col in cols], axis=0)
            k = jnp.exp2(mul(source, target)).astype(jnp.bfloat16)
            d = mul(jnp.concatenate([vec[:, col] for col in cols], axis=1), k)
            acc = d if acc is None else acc + d
        out_ref[:, part(t)] = acc
        return 0

    lax.fori_loop(0, leaf_dev, one, 0)


def near_product(offsets, inverse, left_p, left_v, points, vectors, right_p, right_v):
    dims, count = points.shape
    probes = vectors.shape[0]
    width = count + left_p.shape[1] + right_p.shape[1]
    depth = 4 * dims
    return pl.pallas_call(
        near_kernel,
        in_specs=[pl.BlockSpec(memory_space=pltpu.SMEM)] + vmem(7),
        out_specs=pl.BlockSpec(memory_space=pltpu.VMEM),
        out_shape=jax.ShapeDtypeStruct((probes, count), jnp.float32),
        scratch_shapes=[
            pltpu.VMEM((width, depth), jnp.bfloat16),
            pltpu.VMEM((depth, count), jnp.bfloat16),
            pltpu.VMEM((probes, width), jnp.bfloat16),
        ],
        cost_estimate=pl.CostEstimate(flops=40 * 10**9, bytes_accessed=4 << 20, transcendentals=33 << 20),
        compiler_params=pltpu.CompilerParams(vmem_limit_bytes=32 << 20),
    )(offsets, inverse, left_p, left_v, points, vectors, right_p, right_v)


def far_kernel(
    seg_count, place_ref, local_ref, upper_ref, inv_ref, basis_ref, transfer_ref, up_transfer_ref, up_skeleton_ref,
    own_ref, left_ref, right_ref, top_ref, root_ref, near_ref, out_ref, win, high, src, tgt,
):
    leaf_dev, rank, leaf = basis_ref.shape
    probes = near_ref.shape[0]
    levels = leaf_dev.bit_length()
    cross = seg_count.bit_length() - 3
    pad = CPL_REACH
    place = place_ref[0]
    high[...] = jnp.zeros_like(high)
    at = 0
    edge = 0
    store = 0
    offset = 0
    starts = []
    for height in range(levels):
        boxes = leaf_dev >> height
        row = first_box(leaf_dev, height)
        starts.append(at)
        if boxes >= pad:
            win[at : at + pad] = left_ref[edge : edge + pad]
            win[at + pad : at + pad + boxes] = own_ref[row : row + boxes]
            win[at + pad + boxes : at + 2 * pad + boxes] = right_ref[edge : edge + pad]
            edge += pad
        else:
            for g in range(seg_count):
                spot = store + pad + g * boxes
                high[spot : spot + boxes] = top_ref[g, offset : offset + boxes]
            win[at : at + 2 * pad + boxes] = high[pl.ds(store + place * boxes, 2 * pad + boxes)]
            offset += boxes
            if height < levels - 1:
                store += 2 * pad + boxes * seg_count
        at += 2 * pad + boxes
    for above in range(1, cross + 1):
        boxes = seg_count >> above
        row = 2 * seg_count - 4 * boxes
        skel_row = seg_count - 2 * boxes
        below = store + pad
        store += 2 * pad + 2 * boxes
        for b in range(boxes):
            pair = [root_ref[i] if above == 1 else high[below + i, 0:probes, :] for i in (2 * b, 2 * b + 1)]
            c = mul(pair[0], up_transfer_ref[row + 2 * b]) + mul(pair[1], up_transfer_ref[row + 2 * b + 1])
            high[store + pad + b, 0:probes, :] = c.astype(jnp.bfloat16)
            high[store + pad + b, probes:, :] = up_skeleton_ref[skel_row + b]
        starts.append(at)
        win[at : at + 2 * pad + 1] = high[pl.ds(store + place // (1 << above), 2 * pad + 1)]
        at += 2 * pad + 1
    inv = inv_ref[...]
    for r in range(at):
        s, t = augment(win[r, probes:, :], inv)
        src[r * rank : (r + 1) * rank, :] = s.T
        tgt[r] = t

    def coupled(base, list_ref, row):
        picks = [base + list_ref[row, m] for m in range(list_ref.shape[1])]
        stacked = jnp.concatenate([src[pl.ds(pl.multiple_of(p * rank, rank), rank), :] for p in picks], axis=0)
        k = jnp.exp2(mul(stacked, tgt[base])).astype(jnp.bfloat16)
        total = None
        for m, p in enumerate(picks):
            d = mul(win[p, 0:probes, :], k[m * rank : (m + 1) * rank])
            total = d if total is None else total + d
        return total

    field = None
    for above in range(cross, 0, -1):
        boxes = seg_count >> above
        position = place // (1 << above)
        own = coupled(starts[levels - 1 + above] + pad, upper_ref, seg_count - 2 * boxes + position)
        if field is not None:
            own = own + mul(field, up_transfer_ref[2 * seg_count - 2 * boxes + position], NT)
        field = own.astype(jnp.bfloat16)
    spread = mul(field, up_transfer_ref[place], NT)
    fields = None
    for height in range(levels - 1, -1, -1):
        boxes = leaf_dev >> height
        row = first_box(leaf_dev, height)
        now = []
        for b in range(boxes):
            own = coupled(starts[height] + pad + b, local_ref, row + b)
            if fields is None:
                own = own + spread
            else:
                own = own + mul(fields[b // 2], transfer_ref[row + b], NT)
            now.append(own.astype(jnp.bfloat16))
        fields = now
    for t in range(leaf_dev):
        cols = slice(t * leaf, (t + 1) * leaf)
        out_ref[:, cols] = near_ref[:, cols] + mul(fields[t], basis_ref[t])


def far_sum(
    seg_count, place, local_coupling, upper_coupling, inverse, leaf_basis, local_transfer, upper_transfer,
    upper_skeleton, own, left, right, top, root, near_part,
):
    leaf_dev, rank, _ = leaf_basis.shape
    rows = own.shape[1]
    dims = upper_skeleton.shape[1]
    pad = 2 * CPL_REACH
    counts = [leaf_dev >> h for h in range(leaf_dev.bit_length())]
    uppers = [seg_count >> a for a in range(1, seg_count.bit_length() - 2)]
    window = sum(n + pad for n in counts) + len(uppers) * (pad + 1)
    high = sum(n * seg_count + pad for n in counts if n < CPL_REACH) + sum(n + pad for n in uppers)
    return pl.pallas_call(
        functools.partial(far_kernel, seg_count),
        in_specs=[pl.BlockSpec(memory_space=pltpu.SMEM)] * 3 + vmem(11),
        out_specs=pl.BlockSpec(memory_space=pltpu.VMEM),
        out_shape=jax.ShapeDtypeStruct(near_part.shape, jnp.float32),
        scratch_shapes=[
            pltpu.VMEM((window, rows, rank), jnp.bfloat16),
            pltpu.VMEM((high, rows, rank), jnp.bfloat16),
            pltpu.VMEM((window * rank, 4 * dims), jnp.bfloat16),
            pltpu.VMEM((window, 4 * dims, rank), jnp.bfloat16),
        ],
        cost_estimate=pl.CostEstimate(flops=10**10, bytes_accessed=6 << 20, transcendentals=1 << 20),
        compiler_params=pltpu.CompilerParams(vmem_limit_bytes=40 << 20),
    )(
        place, local_coupling, upper_coupling, inverse, leaf_basis, local_transfer, upper_transfer, upper_skeleton,
        own, left, right, top, root, near_part,
    )


def body(
    points,
    vectors,
    lengthscale,
    leaf_basis,
    local_transfer,
    upper_transfer,
    local_skeleton,
    upper_skeleton,
    near_offsets,
    local_coupling,
    upper_coupling,
):
    inverse = (1.0 / lengthscale)[:, None]
    seg_count = lax.axis_size("seg")
    place = lax.axis_index("seg").astype(jnp.int32)[None]
    own, left_p, left_v, right_p, right_v, far_left, far_right, far_top, far_root = upward(
        seg_count, leaf_basis, points, vectors, local_transfer, local_skeleton
    )
    near_part = near_product(near_offsets, inverse, left_p, left_v, points, vectors, right_p, right_v)
    return far_sum(
        seg_count, place, local_coupling, upper_coupling, inverse, leaf_basis, local_transfer, upper_transfer,
        upper_skeleton, own, far_left, far_right, far_top, far_root, near_part,
    )


def solution(mesh):
    in_specs = (
        P(None, ("groups", "seg")),
        P(None, ("groups", "seg")),
        P("groups"),
        P(("groups", "seg"), None, None),
        P(("groups", "seg"), None, None),
        P("groups", None, None),
        P(("groups", "seg"), None, None),
        P("groups", None, None),
        P(("groups", "seg"), None),
        P(("groups", "seg"), None),
        P("groups", None),
    )
    out_specs = P(None, ("groups", "seg"))
    return jax.shard_map(body, mesh=mesh, in_specs=in_specs, out_specs=out_specs, check_vma=False)
```
